32 devices in a mesh: seq: 16 (over z, y, core), head: 2 (over x).
Axes of the slice: x: 2, y: 2, z: 4, core: 2. Of those that a mesh axis runs over, the one named last changes fastest.
Arguments:
- query_key: bfloat16 [8192, 2048], P('seq', 'head'), may hold values from -7 to 7
- values: bfloat16 [8192, 2048], P('seq', 'head'), may hold values from -12 to 12
- out_weight: bfloat16 [2048, 2048], P('head'), may hold values from -0.125 to 0.125
- out_grad: bfloat16 [8192, 2048], P('seq'), may hold values from -12 to 12
- sort_order: int32 [16, 8192], P('head', 'seq'), may hold values from 0 to 8191, as said below
- undo_order: int32 [16, 8192], P('head', 'seq'), may hold values from 0 to 8191, as said below
Outputs:
- projected: bfloat16 [8192, 2048], P('seq', 'head')
- shared_grad: bfloat16 [8192, 2048], P('seq', 'head')
- value_grad: bfloat16 [8192, 2048], P('seq', 'head')
The draws below stay inside these ranges and needn't reach their ends.
Inputs may be any that keep to these rules, and one draw needn't show every extreme that they name: `sort_order`: each row holds every token index once. For every head, among the tokens t with t // 512 = a, at most 48 have bucket positions p with p // 512 = b, for every pair a, b; exactly 48 for some pair. undo_order[h, sort_order[h, p]] = p for every head h and position p.
All inputs are finite; a program needn't handle non-finite values.
Results may differ from the reference program's by a relative error of at most 0.0079.
Values may be sent and summed in bfloat16 or wider, within the bound.
A program may use at most 128 MiB of HBM per device.

```python
import jax
import jax.numpy as jnp
from jax import lax

H = 16
DH = 128
GROUP = 256
TOK_DEV = 512
D = 2048
SEQ = 8192


def bucket_tables(key):
    devices = SEQ // TOK_DEV
    mean_load = TOK_DEV // devices
    spread = mean_load // 2
    head_keys = jax.random.split(key, H)

    def shuffle_one(shuffle_key):
        return jax.random.permutation(shuffle_key, TOK_DEV)

    def one_head(head_key):
        key_parts = jax.random.split(head_key, 5)
        offsets = jax.random.permutation(key_parts[0], devices)
        lift_sizes = jax.random.randint(key_parts[1], (devices // 2,), 0, spread + 1)
        lift_sizes = lift_sizes.at[0].set(spread)
        pair_loads = jnp.zeros((devices,), jnp.int32)
        pair_loads = pair_loads.at[offsets[0::2]].set(mean_load + lift_sizes)
        pair_loads = pair_loads.at[offsets[1::2]].set(mean_load - lift_sizes)
        mixing = jax.random.permutation(key_parts[2], devices)
        source_ids = jnp.arange(devices)
        counts = pair_loads[(mixing[None, :] - source_ids[:, None]) % devices]
        bounds = jnp.cumsum(counts, axis=1)
        slot_ids = jnp.arange(TOK_DEV)
        targets = jnp.sum((slot_ids[None, :, None] >= bounds[:, None, :]).astype(jnp.int32), axis=2)
        shuffles = jax.vmap(shuffle_one)(jax.random.split(key_parts[3], devices))
        targets = jnp.take_along_axis(targets, shuffles, axis=1).reshape(SEQ)
        tiebreak = jax.random.permutation(key_parts[4], SEQ)
        bucket_order = jnp.argsort(targets * SEQ + tiebreak).astype(jnp.int32)
        inverse = jnp.zeros((SEQ,), jnp.int32).at[bucket_order].set(jnp.arange(SEQ, dtype=jnp.int32))
        return (bucket_order, inverse)
    return jax.vmap(one_head)(head_keys)


def draw_sort_order(key, part):
    return bucket_tables(jax.random.fold_in(key, 11))[0]


def draw_undo_order(key, part):
    return bucket_tables(jax.random.fold_in(key, 11))[1]


def block_levels(rng, shape, pieces, low, largest):
    gain = 1.0
    for position, blocks in pieces:
        steps = jax.random.uniform(jax.random.fold_in(jax.random.fold_in(rng, 6), position), (blocks,), jnp.float32, low / len(pieces), largest / len(pieces))
        gain = gain * jnp.repeat(jnp.exp(steps), shape[position] // blocks).reshape((-1,) + (1,) * (len(shape) - 1 - position))
    return gain


def bell_draw(own_key, shape, deviation, most, pieces=(), kind=jnp.bfloat16):
    gain = block_levels(own_key, shape, pieces, -0.22, 0.18) if pieces else 1.0
    entries = jax.random.normal(own_key, shape, jnp.float32) * deviation * gain
    return jnp.minimum(jnp.maximum(entries, -most), most).astype(kind)


def setup_inputs(seed: int = 0) -> dict:
    seeds = jax.random.split(jax.random.key(seed), 7)
    query_key = bell_draw(seeds[0], (SEQ, D), 1.4, 7.0, ((0, 16), (1, 2)))
    values = bell_draw(seeds[1], (SEQ, D), 2.0, 12.0, ((0, 16), (1, 2)))
    out_weight = bell_draw(seeds[2], (D, D), D ** -0.5, 0.125, ((0, 2),))
    out_grad = bell_draw(seeds[3], (SEQ, D), 2.0, 12.0, ((0, 16),))
    sort_order = draw_sort_order(jax.random.fold_in(seeds[6], 71), 0)
    undo_order = draw_undo_order(jax.random.fold_in(seeds[6], 71), 0)
    return {"query_key": query_key, "values": values, "out_weight": out_weight, "out_grad": out_grad, "sort_order": sort_order, "undo_order": undo_order}


NORM_EPS = 1e-06

def reference(query_key, values, out_weight, out_grad, sort_order, undo_order):
    attended_grad = jnp.dot(out_grad, out_weight.T, preferred_element_type=jnp.float32).astype(jnp.bfloat16)
    head_shape = (SEQ, H, DH)
    query_heads = query_key.reshape(head_shape)
    value_heads = values.reshape(head_shape)
    grad_heads = attended_grad.reshape(head_shape)
    blocks = SEQ // GROUP
    score_scale = DH ** (-0.5)
    keep_mask = jnp.arange(2 * GROUP)[None, :] != jnp.arange(GROUP)[:, None] + GROUP

    def one_head(inputs):
        head_id, order_row, undo_row = inputs

        def pick_rows(table):
            return lax.dynamic_index_in_dim(table, head_id, axis=1, keepdims=False)[order_row]
        sorted_query = pick_rows(query_heads)
        sorted_value = pick_rows(value_heads)
        sorted_grad = pick_rows(grad_heads)
        query_wide = sorted_query.astype(jnp.float32)
        inverse_norm = lax.rsqrt(lax.optimization_barrier(jnp.mean(query_wide * query_wide, axis=1, keepdims=True)) + NORM_EPS)
        key_rows = (query_wide * inverse_norm).astype(jnp.bfloat16)
        query_blocks = query_wide.reshape(blocks, GROUP, DH)
        key_blocks = key_rows.astype(jnp.float32).reshape(blocks, GROUP, DH)
        value_blocks = sorted_value.astype(jnp.float32).reshape(blocks, GROUP, DH)
        grad_blocks = sorted_grad.astype(jnp.float32).reshape(blocks, GROUP, DH)
        key_window = jnp.concatenate([jnp.roll(key_blocks, 1, axis=0), key_blocks], axis=1)
        value_window = jnp.concatenate([jnp.roll(value_blocks, 1, axis=0), value_blocks], axis=1)
        scores = jnp.einsum('nqd,nkd->nqk', query_blocks, key_window) * score_scale
        weights = jnp.where(keep_mask, jnp.exp(scores), 0.0)
        denominator = lax.optimization_barrier(jnp.sum(weights, axis=2, keepdims=True))
        probability = lax.optimization_barrier((weights / denominator).astype(jnp.bfloat16)).astype(jnp.float32)
        out_blocks = jnp.einsum('nqk,nkd->nqd', probability, value_window).astype(jnp.bfloat16)
        prob_grad = jnp.einsum('nqd,nkd->nqk', grad_blocks, value_window)
        row_delta = lax.optimization_barrier(jnp.sum(probability * prob_grad, axis=2, keepdims=True))
        score_grad = lax.optimization_barrier((probability * (prob_grad - row_delta) * score_scale).astype(jnp.bfloat16)).astype(jnp.float32)
        value_window_grad = jnp.einsum('nqk,nqd->nkd', probability, grad_blocks)
        query_grad = jnp.einsum('nqk,nkd->nqd', score_grad, key_window)
        key_window_grad = jnp.einsum('nqk,nqd->nkd', score_grad, query_blocks)
        key_grad = key_window_grad[:, GROUP:] + jnp.roll(key_window_grad[:, :GROUP], -1, axis=0)
        value_sum = value_window_grad[:, GROUP:] + jnp.roll(value_window_grad[:, :GROUP], -1, axis=0)
        sorted_value_grad = value_sum.reshape(SEQ, DH).astype(jnp.bfloat16)
        key_flat = key_grad.reshape(SEQ, DH)
        query_flat = query_grad.reshape(SEQ, DH)
        inner = lax.optimization_barrier(jnp.sum(key_flat * query_wide, axis=1, keepdims=True))
        cubed = inverse_norm * inverse_norm * inverse_norm
        sorted_shared_grad = (query_flat + inverse_norm * key_flat - cubed * query_wide * inner / DH).astype(jnp.bfloat16)
        sorted_out = out_blocks.reshape(SEQ, DH)
        return (sorted_out[undo_row], sorted_shared_grad[undo_row], sorted_value_grad[undo_row])
    results = lax.map(one_head, (jnp.arange(H, dtype=jnp.int32), sort_order, undo_order))
    attended = jnp.transpose(results[0], (1, 0, 2)).reshape(SEQ, D)
    shared_grad = jnp.transpose(results[1], (1, 0, 2)).reshape(SEQ, D)
    value_grad = jnp.transpose(results[2], (1, 0, 2)).reshape(SEQ, D)
    projected = jnp.dot(attended, out_weight, preferred_element_type=jnp.float32).astype(jnp.bfloat16)
    return (projected, shared_grad, value_grad)
```

```python
import functools
import math

import jax
import jax.numpy as jnp
from jax import lax
from jax.experimental import pallas as pl
from jax.experimental.pallas import tpu as pltpu
from jax.sharding import PartitionSpec as P

GROUP = 256
NORM_EPS = 1e-06
MESH = pl.DeviceIdType.MESH
F32 = jnp.float32
BF16 = jnp.bfloat16


def slot_tables(sort_order, undo_order, tok_dev, capacity):
    target = undo_order // tok_dev
    same_target = target[:, :, None] == target[:, None, :]
    before = undo_order[:, None, :] < undo_order[:, :, None]
    outbound = target * capacity + jnp.sum((same_target & before).astype(jnp.int32), axis=2)
    source = sort_order // tok_dev
    same_source = source[:, :, None] == source[:, None, :]
    places = jnp.arange(tok_dev, dtype=jnp.int32)
    earlier = (places[None, :] < places[:, None])[None]
    inbound = source * capacity + jnp.sum((same_source & earlier).astype(jnp.int32), axis=2)
    return outbound, inbound


def dot(a, b, contract):
    return lax.dot_general(a, b, (contract, ((), ())), preferred_element_type=F32)


NN = ((1,), (0,))
NT = ((1,), (1,))
TN = ((0,), (0,))


def kernel(
    n, nh, capacity, head_size,
    qk_ref, v_ref, w_ref, og_ref, out_row, out_col, in_row, in_col,
    proj_ref, dqk_ref, dv_ref,
    send_x, send_g, send_o, recv_x, recv_g, recv_o, recv_d,
    sq, skv, halo, prob, acc_q, acc_k, acc_v, back_send, back,
    att, part_send, part_recv, own,
    sx, rx, sg, rg, so, ro, sd, rd, sh, rh, sb, rb, sp, rp,
):
    tok_dev, _ = qk_ref.shape
    heads = out_row.shape[0]
    slots = n * capacity
    step = math.gcd(slots, 256)
    blocks = tok_dev // GROUP
    scale = head_size ** (-0.5)
    me = lax.axis_index("seq")
    mh = lax.axis_index("head")
    after = lax.rem(me + 1, n)
    ahead = lax.rem(me + n - 1, n)

    barrier = pltpu.get_barrier_semaphore()

    def greet(d, _):
        pl.semaphore_signal(
            barrier, inc=1, device_id={"seq": lax.rem(me + d, n)}, device_id_type=MESH
        )
        return 0

    lax.fori_loop(1, n, greet, 0)
    for e in range(1, nh):
        pl.semaphore_signal(
            barrier, inc=1, device_id={"head": lax.rem(mh + e, nh)}, device_id_type=MESH
        )
    pl.semaphore_wait(barrier, n - 1 + nh - 1)

    def cols(h):
        return pl.ds(pl.multiple_of(h * head_size, head_size), head_size)

    def rows(b):
        return pl.ds(b * GROUP, GROUP)

    def spread(src, dst, h, send_sem, recv_sem):
        mine = pl.ds(pl.multiple_of(me * capacity, 16), capacity)

        def one(d, _):
            peer = lax.rem(me + d, n)
            pltpu.make_async_remote_copy(
                src_ref=src.at[h, pl.ds(pl.multiple_of(peer * capacity, 16), capacity)],
                dst_ref=dst.at[h, mine],
                send_sem=send_sem.at[h],
                recv_sem=recv_sem.at[h],
                device_id={"seq": peer},
                device_id_type=MESH,
            ).start()
            return 0

        lax.fori_loop(1, n, one, 0)
        pltpu.make_async_copy(src.at[h, mine], dst.at[h, mine], recv_sem.at[h]).start()

    def wait_all(ref, sem):
        pltpu.make_async_copy(ref, ref, sem).wait()

    def wait_sent(src, h, sem):
        wait_all(src.at[h, pl.ds(0, slots - capacity)], sem.at[h])

    def pack(row_table, h, values, dst):
        places = row_table[h]
        for c in range(slots // step):
            ids = lax.broadcasted_iota(jnp.int32, (step, tok_dev), 0) + c * step
            pick = jnp.where(ids == places, 1.0, 0.0).astype(BF16)
            dst[h, pl.ds(c * step, step), :] = dot(pick, values, NN).astype(BF16)

    def column(col_table, h, b):
        table = col_table[rows(b), :]
        lane = lax.broadcasted_iota(jnp.int32, table.shape, 1)
        return jnp.sum(jnp.where(lane == h, table, 0.0), axis=1, keepdims=True).astype(jnp.int32)

    def unpack(col_table, h, b, src):
        ids = lax.broadcasted_iota(jnp.int32, (GROUP, slots), 1)
        pick = jnp.where(ids == column(col_table, h, b), 1.0, 0.0).astype(BF16)
        return dot(pick, src[h], NN)

    def inverse_norm(q):
        return lax.rsqrt(jnp.mean(q * q, axis=1, keepdims=True) + NORM_EPS)

    def window(h, b):
        prior = halo[h] if b == 0 else skv[h, rows(b - 1), :]
        both = jnp.concatenate([prior, skv[h, rows(b), :]], axis=0)
        return both[:, :head_size], both[:, head_size:]

    def halo_copy(h):
        return pltpu.make_async_remote_copy(
            src_ref=skv.at[h, rows(blocks - 1)], dst_ref=halo.at[h],
            send_sem=sh.at[h], recv_sem=rh.at[h],
            device_id={"seq": after}, device_id_type=MESH,
        )

    def back_copy(h):
        return pltpu.make_async_remote_copy(
            src_ref=back_send.at[h], dst_ref=back.at[h],
            send_sem=sb.at[h], recv_sem=rb.at[h],
            device_id={"seq": ahead}, device_id_type=MESH,
        )

    def each_head(f):
        def go(h, _):
            f(h)
            return 0

        lax.fori_loop(0, heads, go, 0)

    def send_tokens(h):
        both = jnp.concatenate([qk_ref[:, cols(h)], v_ref[:, cols(h)]], axis=1)
        pack(out_row, h, both, send_x)
        spread(send_x, recv_x, h, sx, rx)

    def sort_tokens(h):
        wait_all(recv_x.at[h], rx.at[h])
        for b in range(blocks):
            arrived = unpack(in_col, h, b, recv_x)
            q = arrived[:, :head_size]
            sq[h, rows(b), :] = q.astype(BF16)
            skv[h, rows(b), :head_size] = (q * inverse_norm(q)).astype(BF16)
            skv[h, rows(b), head_size:] = arrived[:, head_size:].astype(BF16)
        halo_copy(h).start()
        grad = dot(og_ref[...], w_ref[cols(h), :], NT).astype(BF16)
        pack(out_row, h, grad, send_g)
        spread(send_g, recv_g, h, sg, rg)

    def forward(h):
        halo_copy(h).wait_recv()
        outs = []
        for b in range(blocks):
            keys, vals = window(h, b)
            scores = dot(sq[h, rows(b), :], keys, NT) * scale
            own_id = lax.broadcasted_iota(jnp.int32, scores.shape, 0) + GROUP
            other = lax.broadcasted_iota(jnp.int32, scores.shape, 1)
            weights = jnp.where(own_id != other, jnp.exp(scores), 0.0)
            probability = (weights / jnp.sum(weights, axis=1, keepdims=True)).astype(BF16)
            prob[h, rows(b), :] = probability
            outs.append(dot(probability, vals, NN).astype(BF16))
        pack(in_row, h, jnp.concatenate(outs, axis=0), send_o)
        spread(send_o, recv_o, h, so, ro)

    def backward(h):
        wait_all(recv_g.at[h], rg.at[h])
        for b in range(blocks):
            keys, vals = window(h, b)
            grad = unpack(in_col, h, b, recv_g).astype(BF16)
            probability = prob[h, rows(b), :]
            wide = probability.astype(F32)
            prob_grad = dot(grad, vals, NT)
            delta = jnp.sum(wide * prob_grad, axis=1, keepdims=True)
            score_grad = (wide * (prob_grad - delta) * scale).astype(BF16)
            acc_q[h, rows(b), :] = dot(score_grad, keys, NN)
            v_part = dot(probability, grad, TN)
            k_part = dot(score_grad, sq[h, rows(b), :], TN)
            if b == 0:
                back_send[h, :, :head_size] = k_part[:GROUP].astype(BF16)
                back_send[h, :, head_size:] = v_part[:GROUP].astype(BF16)
                back_copy(h).start()
            else:
                acc_k[h, rows(b - 1), :] += k_part[:GROUP]
                acc_v[h, rows(b - 1), :] += v_part[:GROUP]
            acc_k[h, rows(b), :] = k_part[GROUP:]
            acc_v[h, rows(b), :] = v_part[GROUP:]

    def finish(h):
        back_copy(h).wait_recv()
        wait_sent(send_x, h, sx)
        done = []
        for b in range(blocks):
            k_grad = acc_k[h, rows(b), :]
            v_grad = acc_v[h, rows(b), :]
            if b == blocks - 1:
                k_grad += back[h, :, :head_size].astype(F32)
                v_grad += back[h, :, head_size:].astype(F32)
            q = sq[h, rows(b), :].astype(F32)
            norm = inverse_norm(q)
            inner = jnp.sum(k_grad * q, axis=1, keepdims=True) / head_size
            shared = acc_q[h, rows(b), :] + norm * k_grad - norm * norm * norm * inner * q
            done.append(jnp.concatenate([shared.astype(BF16), v_grad.astype(BF16)], axis=1))
        pack(in_row, h, jnp.concatenate(done, axis=0), send_x)
        spread(send_x, recv_d, h, sd, rd)

    def collect_out(h):
        wait_all(recv_o.at[h], ro.at[h])
        for b in range(blocks):
            att[rows(b), cols(h)] = unpack(out_col, h, b, recv_o).astype(BF16)

    def collect_grads(h):
        wait_all(recv_d.at[h], rd.at[h])
        for b in range(blocks):
            arrived = unpack(out_col, h, b, recv_d).astype(BF16)
            dqk_ref[rows(b), cols(h)] = arrived[:, :head_size]
            dv_ref[rows(b), cols(h)] = arrived[:, head_size:]

    each_head(send_tokens)
    each_head(sort_tokens)
    each_head(forward)
    each_head(backward)
    each_head(finish)
    each_head(collect_out)

    width = proj_ref.shape[1]
    tile = math.gcd(width, 256)

    def project(owner, write):
        def go(c, _):
            at = pl.multiple_of(c * tile, tile)
            taken = pl.ds(pl.multiple_of(owner * width + c * tile, tile), tile)
            write(pl.ds(at, tile), dot(att[...], w_ref[:, taken], NN))
            return 0

        lax.fori_loop(0, width // tile, go, 0)

    def part_copy(e):
        return pltpu.make_async_remote_copy(
            src_ref=part_send.at[e - 1], dst_ref=part_recv.at[e - 1],
            send_sem=sp.at[e - 1], recv_sem=rp.at[e - 1],
            device_id={"head": lax.rem(mh + e, nh)}, device_id_type=MESH,
        )

    for e in range(1, nh):
        def write_part(at, part, e=e):
            part_send[e - 1, :, at] = part.astype(BF16)

        project(lax.rem(mh + e, nh), write_part)
        part_copy(e).start()

    def write_own(at, part):
        own[:, at] = part

    project(mh, write_own)
    each_head(collect_grads)
    for e in range(1, nh):
        part_copy(e).wait_recv()
        own[...] += part_recv[e - 1].astype(F32)
    proj_ref[...] = own[...].astype(BF16)

    def drain(h):
        wait_sent(send_x, h, sd)
        wait_sent(send_g, h, sg)
        wait_sent(send_o, h, so)
        halo_copy(h).wait_send()
        back_copy(h).wait_send()

    each_head(drain)
    for e in range(1, nh):
        part_copy(e).wait_send()


def on_device(query_key, values, out_weight, out_grad, sort_order, undo_order):
    tok_dev, flat_width = query_key.shape
    heads = sort_order.shape[0]
    head_size = flat_width // heads
    n = lax.axis_size("seq")
    nh = lax.axis_size("head")
    most = 3 * tok_dev // (2 * n)
    capacity = (most + 15) // 16 * 16
    slots = n * capacity
    width = out_weight.shape[1] // nh
    outbound, inbound = slot_tables(sort_order, undo_order, tok_dev, capacity)
    vmem = pl.BlockSpec(memory_space=pltpu.VMEM)
    sems = pltpu.SemaphoreType.DMA((heads,))
    shape = jax.ShapeDtypeStruct
    return pl.pallas_call(
        functools.partial(kernel, n, nh, capacity, head_size),
        out_shape=(
            shape((tok_dev, width), BF16),
            shape((tok_dev, flat_width), BF16),
            shape((tok_dev, flat_width), BF16),
        ),
        in_specs=[vmem] * 8,
        out_specs=(vmem, vmem, vmem),
        scratch_shapes=[
            pltpu.VMEM((heads, slots, 2 * head_size), BF16),
            pltpu.VMEM((heads, slots, head_size), BF16),
            pltpu.VMEM((heads, slots, head_size), BF16),
            pltpu.VMEM((heads, slots, 2 * head_size), BF16),
            pltpu.VMEM((heads, slots, head_size), BF16),
            pltpu.VMEM((heads, slots, head_size), BF16),
            pltpu.VMEM((heads, slots, 2 * head_size), BF16),
            pltpu.VMEM((heads, tok_dev, head_size), BF16),
            pltpu.VMEM((heads, tok_dev, 2 * head_size), BF16),
            pltpu.VMEM((heads, GROUP, 2 * head_size), BF16),
            pltpu.VMEM((heads, tok_dev, 2 * GROUP), BF16),
            pltpu.VMEM((heads, tok_dev, head_size), F32),
            pltpu.VMEM((heads, tok_dev, head_size), F32),
            pltpu.VMEM((heads, tok_dev, head_size), F32),
            pltpu.VMEM((heads, GROUP, 2 * head_size), BF16),
            pltpu.VMEM((heads, GROUP, 2 * head_size), BF16),
            pltpu.VMEM((tok_dev, flat_width), BF16),
            pltpu.VMEM((max(nh - 1, 1), tok_dev, width), BF16),
            pltpu.VMEM((max(nh - 1, 1), tok_dev, width), BF16),
            pltpu.VMEM((tok_dev, width), F32),
        ]
        + [sems] * 12
        + [pltpu.SemaphoreType.DMA((max(nh - 1, 1),))] * 2,
        compiler_params=pltpu.CompilerParams(
            collective_id=0, has_side_effects=True, vmem_limit_bytes=62 * 2**20
        ),
        cost_estimate=pl.CostEstimate(
            flops=2 * 10**10, bytes_accessed=2**24, transcendentals=2**21
        ),
    )(
        query_key, values, out_weight, out_grad,
        outbound[:, None, :], outbound.T.astype(F32),
        inbound[:, None, :], inbound.T.astype(F32),
    )


def solution(mesh):
    placed = (
        P("seq", "head"),
        P("seq", "head"),
        P("head", None),
        P("seq", None),
        P("head", "seq"),
        P("head", "seq"),
    )
    return jax.shard_map(
        on_device,
        mesh=mesh,
        in_specs=placed,
        out_specs=(P("seq", "head"), P("seq", "head"), P("seq", "head")),
        check_vma=False,
    )
```

```python
import functools
import math

import jax
import jax.numpy as jnp
from jax import lax
from jax.experimental import pallas as pl
from jax.experimental.pallas import tpu as pltpu
from jax.sharding import PartitionSpec as P

GROUP = 256
NORM_EPS = 1e-06
MESH = pl.DeviceIdType.MESH
F32 = jnp.float32
BF16 = jnp.bfloat16


def quotient(x, by):
    return x >> (by.bit_length() - 1) if by & (by - 1) == 0 else lax.div(x, jnp.int32(by))


def dot(a, b, contract):
    return lax.dot_general(a, b, (contract, ((), ())), preferred_element_type=F32)


NN = ((1,), (0,))
NT = ((1,), (1,))
TN = ((0,), (0,))


def kernel(
    n, nh, capacity, head_size,
    qk_hbm, v_hbm, w_hbm, og_hbm, sort_ref, undo_ref,
    proj_out, dqk_out, dv_out,
    qk_ref, v_ref, w_ref, og_ref, proj_ref, dqk_ref, dv_ref,
    out_row, out_col, in_row, in_col,
    send_x, send_g, send_o, recv_x, recv_g, recv_o, recv_d,
    sq, skv, halo, acc_q, acc_k, acc_v, back_send, back,
    att, part_send, part_recv, own,
    sx, rx, sg, rg, so, ro, sd, rd, sh, rh, sb, rb, oq, ov, sp, rp, load, op,
):
    tok_dev, _ = qk_ref.shape
    heads = out_row.shape[0]
    slots = n * capacity
    step = math.gcd(slots, 256)
    blocks = tok_dev // GROUP
    scale = head_size ** (-0.5)
    me = lax.axis_index("seq")
    mh = lax.axis_index("head")
    after = lax.rem(me + 1, n)
    ahead = lax.rem(me + n - 1, n)

    barrier = pltpu.get_barrier_semaphore()

    def greet(d, _):
        pl.semaphore_signal(
            barrier, inc=1, device_id={"seq": lax.rem(me + d, n)}, device_id_type=MESH
        )
        return 0

    lax.fori_loop(1, n, greet, 0)
    for e in range(1, nh):
        pl.semaphore_signal(
            barrier, inc=1, device_id={"head": lax.rem(mh + e, nh)}, device_id_type=MESH
        )
    loads = [
        pltpu.make_async_copy(src, dst, load.at[i])
        for i, (src, dst) in enumerate(
            [(qk_hbm, qk_ref), (v_hbm, v_ref), (w_hbm, w_ref), (og_hbm, og_ref)]
        )
    ]
    for copy in loads:
        copy.start()
    out_col[...] = jnp.zeros_like(out_col)
    in_col[...] = jnp.zeros_like(in_col)

    def cols(h):
        return pl.ds(pl.multiple_of(h * head_size, head_size), head_size)

    def rows(b):
        return pl.ds(b * GROUP, GROUP)

    def spread(src, dst, h, send_sem, recv_sem):
        mine = pl.ds(pl.multiple_of(me * capacity, 16), capacity)

        def one(d, _):
            peer = lax.rem(me + d, n)
            pltpu.make_async_remote_copy(
                src_ref=src.at[h, pl.ds(pl.multiple_of(peer * capacity, 16), capacity)],
                dst_ref=dst.at[h, mine],
                send_sem=send_sem.at[h],
                recv_sem=recv_sem.at[h],
                device_id={"seq": peer},
                device_id_type=MESH,
            ).start()
            return 0

        lax.fori_loop(1, n, one, 0)
        pltpu.make_async_copy(src.at[h, mine], dst.at[h, mine], recv_sem.at[h]).start()

    def wait_all(ref, sem):
        pltpu.make_async_copy(ref, ref, sem).wait()

    def wait_sent(src, h, sem):
        wait_all(src.at[h, pl.ds(0, slots - capacity)], sem.at[h])

    def pack(row_table, h, values, dst):
        places = row_table[h]
        for c in range(slots // step):
            ids = lax.broadcasted_iota(jnp.int32, (step, tok_dev), 0) + c * step
            pick = jnp.where(ids == places, 1.0, 0.0).astype(BF16)
            dst[h, pl.ds(c * step, step), :] = dot(pick, values, NN).astype(BF16)

    square = (tok_dev, tok_dev)

    def down():
        return lax.broadcasted_iota(jnp.int32, square, 0)

    def across():
        return lax.broadcasted_iota(jnp.int32, square, 1)

    def count(mask, axis):
        return jnp.sum(jnp.where(mask, 1.0, 0.0), axis=axis, keepdims=True)

    def as_column(row):
        picked = jnp.where(down() == across(), row.astype(F32), 0.0)
        return jnp.sum(picked, axis=1, keepdims=True).astype(jnp.int32)

    def put(row_table, col_table, h, row, col):
        row_table[h] = row.astype(jnp.int32)
        lane = lax.broadcasted_iota(jnp.int32, col_table.shape, 1)
        col_table[...] = jnp.where(lane == h, col, col_table[...])

    def send_slots(h):
        row = undo_ref[pl.ds(h, 1), :]
        col = as_column(row)
        to_row, to_col = quotient(row, tok_dev), quotient(col, tok_dev)
        same = to_row == to_col
        put(
            out_row, out_col, h,
            (to_row * capacity).astype(F32) + count(same & (col < row), 0),
            (to_col * capacity).astype(F32) + count(same & (row < col), 1),
        )

    def arrival_slots(h):
        row = quotient(sort_ref[pl.ds(h, 1), :], tok_dev)
        col = as_column(row)
        same = row == col
        put(
            in_row, in_col, h,
            (row * capacity).astype(F32) + count(same & (down() < across()), 0),
            (col * capacity).astype(F32) + count(same & (across() < down()), 1),
        )

    def column(col_table, h, b):
        table = col_table[rows(b), :]
        lane = lax.broadcasted_iota(jnp.int32, table.shape, 1)
        return jnp.sum(jnp.where(lane == h, table, 0.0), axis=1, keepdims=True).astype(jnp.int32)

    def unpack(col_table, h, b, src):
        ids = lax.broadcasted_iota(jnp.int32, (GROUP, slots), 1)
        pick = jnp.where(ids == column(col_table, h, b), 1.0, 0.0).astype(BF16)
        return dot(pick, src[h], NN)

    def inverse_norm(q):
        return lax.rsqrt(jnp.mean(q * q, axis=1, keepdims=True) + NORM_EPS)

    def window(h, b):
        prior = halo[h] if b == 0 else skv[h, rows(b - 1), :]
        both = jnp.concatenate([prior, skv[h, rows(b), :]], axis=0)
        return both[:, :head_size], both[:, head_size:]

    def halo_copy(h):
        return pltpu.make_async_remote_copy(
            src_ref=skv.at[h, rows(blocks - 1)], dst_ref=halo.at[h],
            send_sem=sh.at[h], recv_sem=rh.at[h],
            device_id={"seq": after}, device_id_type=MESH,
        )

    def back_copy(h):
        return pltpu.make_async_remote_copy(
            src_ref=back_send.at[h], dst_ref=back.at[h],
            send_sem=sb.at[h], recv_sem=rb.at[h],
            device_id={"seq": ahead}, device_id_type=MESH,
        )

    def each_head(f, first=0, last=heads):
        def go(h, _):
            f(h)
            return 0

        lax.fori_loop(first, last, go, 0)

    def pack_tokens(h):
        both = jnp.concatenate([qk_ref[:, cols(h)], v_ref[:, cols(h)]], axis=1)
        pack(out_row, h, both, send_x)

    def send_tokens(h):
        send_slots(h)
        pack_tokens(h)
        spread(send_x, recv_x, h, sx, rx)

    def sort_tokens(h):
        arrival_slots(h)
        wait_all(recv_x.at[h], rx.at[h])
        for b in range(blocks):
            arrived = unpack(in_col, h, b, recv_x)
            q = arrived[:, :head_size]
            sq[h, rows(b), :] = q.astype(BF16)
            skv[h, rows(b), :head_size] = (q * inverse_norm(q)).astype(BF16)
            skv[h, rows(b), head_size:] = arrived[:, head_size:].astype(BF16)
        halo_copy(h).start()
        grad = dot(og_ref[...], w_ref[cols(h), :], NT).astype(BF16)
        pack(out_row, h, grad, send_g)
        spread(send_g, recv_g, h, sg, rg)

    def attend(h):
        halo_copy(h).wait_recv()
        wait_all(recv_g.at[h], rg.at[h])
        outs = []
        for b in range(blocks):
            keys, vals = window(h, b)
            q = sq[h, rows(b), :]
            scores = dot(q, keys, NT) * scale
            own_id = lax.broadcasted_iota(jnp.int32, scores.shape, 0) + GROUP
            other = lax.broadcasted_iota(jnp.int32, scores.shape, 1)
            weights = jnp.where(own_id != other, jnp.exp(scores), 0.0)
            probability = (weights / jnp.sum(weights, axis=1, keepdims=True)).astype(BF16)
            outs.append(dot(probability, vals, NN).astype(BF16))
            grad = unpack(in_col, h, b, recv_g).astype(BF16)
            wide = probability.astype(F32)
            prob_grad = dot(grad, vals, NT)
            delta = jnp.sum(wide * prob_grad, axis=1, keepdims=True)
            score_grad = (wide * (prob_grad - delta) * scale).astype(BF16)
            acc_q[h, rows(b), :] = dot(score_grad, keys, NN)
            v_part = dot(probability, grad, TN)
            k_part = dot(score_grad, q, TN)
            if b == 0:
                back_send[h, :, :head_size] = k_part[:GROUP].astype(BF16)
                back_send[h, :, head_size:] = v_part[:GROUP].astype(BF16)
                back_copy(h).start()
            else:
                acc_k[h, rows(b - 1), :] += k_part[:GROUP]
                acc_v[h, rows(b - 1), :] += v_part[:GROUP]
            acc_k[h, rows(b), :] = k_part[GROUP:]
            acc_v[h, rows(b), :] = v_part[GROUP:]
        pack(in_row, h, jnp.concatenate(outs, axis=0), send_o)
        spread(send_o, recv_o, h, so, ro)

    def finish(h):
        back_copy(h).wait_recv()
        wait_sent(send_x, h, sx)
        done = []
        for b in range(blocks):
            k_grad = acc_k[h, rows(b), :]
            v_grad = acc_v[h, rows(b), :]
            if b == blocks - 1:
                k_grad += back[h, :, :head_size].astype(F32)
                v_grad += back[h, :, head_size:].astype(F32)
            q = sq[h, rows(b), :].astype(F32)
            norm = inverse_norm(q)
            inner = jnp.sum(k_grad * q, axis=1, keepdims=True) / head_size
            shared = acc_q[h, rows(b), :] + norm * k_grad - norm * norm * norm * inner * q
            done.append(jnp.concatenate([shared.astype(BF16), v_grad.astype(BF16)], axis=1))
        pack(in_row, h, jnp.concatenate(done, axis=0), send_x)
        spread(send_x, recv_d, h, sd, rd)

    def collect_out(h):
        wait_all(recv_o.at[h], ro.at[h])
        for b in range(blocks):
            att[rows(b), cols(h)] = unpack(out_col, h, b, recv_o).astype(BF16)

    def collect_grads(h):
        wait_all(recv_d.at[h], rd.at[h])
        for b in range(blocks):
            arrived = unpack(out_col, h, b, recv_d).astype(BF16)
            dqk_ref[rows(b), cols(h)] = arrived[:, :head_size]
            dv_ref[rows(b), cols(h)] = arrived[:, head_size:]
        for copy in grad_copies(h):
            copy.start()

    def grad_copies(h):
        at = (slice(None), cols(h))
        return (
            pltpu.make_async_copy(dqk_ref.at[at], dqk_out.at[at], oq.at[h]),
            pltpu.make_async_copy(dv_ref.at[at], dv_out.at[at], ov.at[h]),
        )

    send_slots(0)
    loads[0].wait()
    loads[1].wait()
    pack_tokens(0)
    pl.semaphore_wait(barrier, n - 1 + nh - 1)
    spread(send_x, recv_x, 0, sx, rx)
    each_head(send_tokens, 1)
    loads[2].wait()
    loads[3].wait()
    each_head(sort_tokens)
    lag = heads // 2

    def attend_and_finish(h):
        attend(h)
        finish(h - lag)

    each_head(attend, 0, lag)
    each_head(attend_and_finish, lag)
    each_head(finish, heads - lag)
    each_head(collect_out)

    width = proj_ref.shape[1]
    tile = math.gcd(width, 256)

    def project(owner, write):
        def go(c, _):
            at = pl.multiple_of(c * tile, tile)
            taken = pl.ds(pl.multiple_of(owner * width + c * tile, tile), tile)
            write(pl.ds(at, tile), dot(att[...], w_ref[:, taken], NN))
            return 0

        lax.fori_loop(0, width // tile, go, 0)

    def part_copy(e):
        return pltpu.make_async_remote_copy(
            src_ref=part_send.at[e - 1], dst_ref=part_recv.at[e - 1],
            send_sem=sp.at[e - 1], recv_sem=rp.at[e - 1],
            device_id={"head": lax.rem(mh + e, nh)}, device_id_type=MESH,
        )

    for e in range(1, nh):
        def write_part(at, part, e=e):
            part_send[e - 1, :, at] = part.astype(BF16)

        project(lax.rem(mh + e, nh), write_part)
        part_copy(e).start()

    def write_own(at, part):
        own[:, at] = part

    project(mh, write_own)
    each_head(collect_grads, 0, heads - 1)
    for e in range(1, nh):
        part_copy(e).wait_recv()
        own[...] += part_recv[e - 1].astype(F32)
    proj_ref[...] = own[...].astype(BF16)
    proj_copy = pltpu.make_async_copy(proj_ref, proj_out, op.at[0])
    proj_copy.start()
    collect_grads(heads - 1)

    def drain(h):
        for copy in grad_copies(h):
            copy.wait()
        wait_sent(send_x, h, sd)
        wait_sent(send_g, h, sg)
        wait_sent(send_o, h, so)
        halo_copy(h).wait_send()
        back_copy(h).wait_send()

    each_head(drain)
    for e in range(1, nh):
        part_copy(e).wait_send()
    proj_copy.wait()


def hand_over(parts, *refs):
    count = (len(refs) - 1) // 2
    sems = refs[-1]
    copies = []
    for i in range(count):
        length = refs[i].shape[0] // parts
        for c in range(parts):
            at = pl.ds(c * length, length)
            copies.append(
                pltpu.make_async_copy(
                    refs[i].at[at], refs[count + i].at[at], sems.at[i * parts + c]
                )
            )
    for copy in copies:
        copy.start()
    for copy in copies:
        copy.wait()


def on_device(query_key, values, out_weight, out_grad, sort_order, undo_order):
    tok_dev, flat_width = query_key.shape
    heads = sort_order.shape[0]
    head_size = flat_width // heads
    n = lax.axis_size("seq")
    nh = lax.axis_size("head")
    most = 3 * tok_dev // (2 * n)
    capacity = (most + 15) // 16 * 16
    slots = n * capacity
    width = out_weight.shape[1] // nh
    vmem = pl.BlockSpec(memory_space=pltpu.VMEM)
    sems = pltpu.SemaphoreType.DMA((heads,))
    anywhere = pl.BlockSpec(memory_space=pl.ANY)
    shape = jax.ShapeDtypeStruct
    results = pl.pallas_call(
        functools.partial(kernel, n, nh, capacity, head_size),
        out_shape=(
            shape((tok_dev, width), BF16),
            shape((tok_dev, flat_width), BF16),
            shape((tok_dev, flat_width), BF16),
        ),
        in_specs=[anywhere] * 4 + [vmem] * 2,
        out_specs=(anywhere,) * 3,
        scratch_shapes=[
            pltpu.VMEM(query_key.shape, BF16),
            pltpu.VMEM(values.shape, BF16),
            pltpu.VMEM(out_weight.shape, BF16),
            pltpu.VMEM(out_grad.shape, BF16),
            pltpu.VMEM((tok_dev, width), BF16),
            pltpu.VMEM((tok_dev, flat_width), BF16),
            pltpu.VMEM((tok_dev, flat_width), BF16),
            pltpu.VMEM((heads, 1, tok_dev), jnp.int32),
            pltpu.VMEM((tok_dev, heads), F32),
            pltpu.VMEM((heads, 1, tok_dev), jnp.int32),
            pltpu.VMEM((tok_dev, heads), F32),
            pltpu.VMEM((heads, slots, 2 * head_size), BF16),
            pltpu.VMEM((heads, slots, head_size), BF16),
            pltpu.VMEM((heads, slots, head_size), BF16),
            pltpu.VMEM((heads, slots, 2 * head_size), BF16),
            pltpu.VMEM((heads, slots, head_size), BF16),
            pltpu.VMEM((heads, slots, head_size), BF16),
            pltpu.VMEM((heads, slots, 2 * head_size), BF16),
            pltpu.VMEM((heads, tok_dev, head_size), BF16),
            pltpu.VMEM((heads, tok_dev, 2 * head_size), BF16),
            pltpu.VMEM((heads, GROUP, 2 * head_size), BF16),
            pltpu.VMEM((heads, tok_dev, head_size), F32),
            pltpu.VMEM((heads, tok_dev, head_size), F32),
            pltpu.VMEM((heads, tok_dev, head_size), F32),
            pltpu.VMEM((heads, GROUP, 2 * head_size), BF16),
            pltpu.VMEM((heads, GROUP, 2 * head_size), BF16),
            pltpu.VMEM((tok_dev, flat_width), BF16),
            pltpu.VMEM((max(nh - 1, 1), tok_dev, width), BF16),
            pltpu.VMEM((max(nh - 1, 1), tok_dev, width), BF16),
            pltpu.VMEM((tok_dev, width), F32),
        ]
        + [sems] * 14
        + [pltpu.SemaphoreType.DMA((max(nh - 1, 1),))] * 2
        + [pltpu.SemaphoreType.DMA((4,)), pltpu.SemaphoreType.DMA((1,))],
        compiler_params=pltpu.CompilerParams(
            collective_id=0, has_side_effects=True, vmem_limit_bytes=62 * 2**20
        ),
        cost_estimate=pl.CostEstimate(
            flops=2 * 10**10, bytes_accessed=2**24, transcendentals=2**21
        ),
    )(
        query_key, values, out_weight, out_grad, sort_order, undo_order
    )
    parts = 4
    return pl.pallas_call(
        functools.partial(hand_over, parts),
        out_shape=tuple(shape(r.shape, r.dtype) for r in results),
        in_specs=[anywhere] * 3,
        out_specs=(anywhere,) * 3,
        scratch_shapes=[pltpu.SemaphoreType.DMA((3 * parts,))],
        cost_estimate=pl.CostEstimate(
            flops=0, bytes_accessed=6 * values.size * 2, transcendentals=0
        ),
    )(*results)


def solution(mesh):
    placed = (
        P("seq", "head"),
        P("seq", "head"),
        P("head", None),
        P("seq", None),
        P("head", "seq"),
        P("head", "seq"),
    )
    return jax.shard_map(
        on_device,
        mesh=mesh,
        in_specs=placed,
        out_specs=(P("seq", "head"), P("seq", "head"), P("seq", "head")),
        check_vma=False,
    )
```

```python
import functools
import math

import jax
import jax.numpy as jnp
from jax import lax
from jax.experimental import pallas as pl
from jax.experimental.pallas import tpu as pltpu
from jax.sharding import PartitionSpec as P

GROUP = 256
NORM_EPS = 1e-06
MESH = pl.DeviceIdType.MESH
F32 = jnp.float32
BF16 = jnp.bfloat16


def quotient(x, by):
    return x >> (by.bit_length() - 1) if by & (by - 1) == 0 else lax.div(x, jnp.int32(by))


def dot(a, b, contract):
    return lax.dot_general(a, b, (contract, ((), ())), preferred_element_type=F32)


NN = ((1,), (0,))
NT = ((1,), (1,))
TN = ((0,), (0,))


def kernel(
    n, nh, capacity, head_size,
    qk_hbm, v_hbm, w_hbm, og_hbm, sort_ref, undo_ref,
    proj_out, dqk_out, dv_out,
    qk_ref, v_ref, w_ref, og_ref, proj_ref, dqk_ref, dv_ref,
    out_row, out_col, in_row, in_col,
    send_x, send_g, send_o, recv_x, recv_g, recv_o, recv_d,
    sq, skv, halo, acc_q, acc_k, acc_v, back_send, back,
    att, part_send, part_recv, own,
    sx, rx, sg, rg, so, ro, sd, rd, sh, rh, sb, rb, oq, ov, sp, rp, load, op,
):
    tok_dev, _ = qk_ref.shape
    heads = out_row.shape[0]
    slots = n * capacity
    step = math.gcd(slots, 256)
    blocks = tok_dev // GROUP
    scale = head_size ** (-0.5)
    me = lax.axis_index("seq")
    mh = lax.axis_index("head")
    after = lax.rem(me + 1, n)
    ahead = lax.rem(me + n - 1, n)

    barrier = pltpu.get_barrier_semaphore()

    def greet(d, _):
        pl.semaphore_signal(
            barrier, inc=1, device_id={"seq": lax.rem(me + d, n)}, device_id_type=MESH
        )
        return 0

    lax.fori_loop(1, n, greet, 0)
    for e in range(1, nh):
        pl.semaphore_signal(
            barrier, inc=1, device_id={"head": lax.rem(mh + e, nh)}, device_id_type=MESH
        )
    loads = [
        pltpu.make_async_copy(src, dst, load.at[i])
        for i, (src, dst) in enumerate(
            [(qk_hbm, qk_ref), (v_hbm, v_ref), (w_hbm, w_ref), (og_hbm, og_ref)]
        )
    ]
    for copy in loads:
        copy.start()
    out_col[...] = jnp.zeros_like(out_col)
    in_col[...] = jnp.zeros_like(in_col)

    def cols(h):
        return pl.ds(pl.multiple_of(h * head_size, head_size), head_size)

    def rows(b):
        return pl.ds(b * GROUP, GROUP)

    def spread(src, dst, h, send_sem, recv_sem):
        mine = pl.ds(pl.multiple_of(me * capacity, 16), capacity)

        def one(i, _):
            peer = lax.rem(me + i // 2 + (i % 2) * (n // 2), n)
            pltpu.make_async_remote_copy(
                src_ref=src.at[h, pl.ds(pl.multiple_of(peer * capacity, 16), capacity)],
                dst_ref=dst.at[h, mine],
                send_sem=send_sem.at[h],
                recv_sem=recv_sem.at[h],
                device_id={"seq": peer},
                device_id_type=MESH,
            ).start()
            return 0

        lax.fori_loop(1, n, one, 0)
        pltpu.make_async_copy(src.at[h, mine], dst.at[h, mine], recv_sem.at[h]).start()

    def wait_all(ref, sem):
        pltpu.make_async_copy(ref, ref, sem).wait()

    def wait_sent(src, h, sem):
        wait_all(src.at[h, pl.ds(0, slots - capacity)], sem.at[h])

    def pack(row_table, h, values, dst):
        places = row_table[h]
        for c in range(slots // step):
            ids = lax.broadcasted_iota(jnp.int32, (step, tok_dev), 0) + c * step
            pick = jnp.where(ids == places, 1.0, 0.0).astype(BF16)
            dst[h, pl.ds(c * step, step), :] = dot(pick, values, NN).astype(BF16)

    square = (tok_dev, tok_dev)

    def down():
        return lax.broadcasted_iota(jnp.int32, square, 0)

    def across():
        return lax.broadcasted_iota(jnp.int32, square, 1)

    def count(mask, axis):
        return jnp.sum(jnp.where(mask, 1.0, 0.0), axis=axis, keepdims=True)

    def as_column(row):
        picked = jnp.where(down() == across(), row.astype(F32), 0.0)
        return jnp.sum(picked, axis=1, keepdims=True).astype(jnp.int32)

    def put(row_table, col_table, h, row, col):
        row_table[h] = row.astype(jnp.int32)
        lane = lax.broadcasted_iota(jnp.int32, col_table.shape, 1)
        col_table[...] = jnp.where(lane == h, col, col_table[...])

    def send_slots(h):
        row = undo_ref[pl.ds(h, 1), :]
        col = as_column(row)
        to_row, to_col = quotient(row, tok_dev), quotient(col, tok_dev)
        same = to_row == to_col
        put(
            out_row, out_col, h,
            (to_row * capacity).astype(F32) + count(same & (col < row), 0),
            (to_col * capacity).astype(F32) + count(same & (row < col), 1),
        )

    def arrival_slots(h):
        row = quotient(sort_ref[pl.ds(h, 1), :], tok_dev)
        col = as_column(row)
        same = row == col
        put(
            in_row, in_col, h,
            (row * capacity).astype(F32) + count(same & (down() < across()), 0),
            (col * capacity).astype(F32) + count(same & (across() < down()), 1),
        )

    def column(col_table, h, b):
        table = col_table[rows(b), :]
        lane = lax.broadcasted_iota(jnp.int32, table.shape, 1)
        return jnp.sum(jnp.where(lane == h, table, 0.0), axis=1, keepdims=True).astype(jnp.int32)

    def unpack(col_table, h, b, src):
        ids = lax.broadcasted_iota(jnp.int32, (GROUP, slots), 1)
        pick = jnp.where(ids == column(col_table, h, b), 1.0, 0.0).astype(BF16)
        return dot(pick, src[h], NN)

    def inverse_norm(q):
        return lax.rsqrt(jnp.mean(q * q, axis=1, keepdims=True) + NORM_EPS)

    def window(h, b):
        prior = halo[h] if b == 0 else skv[h, rows(b - 1), :]
        both = jnp.concatenate([prior, skv[h, rows(b), :]], axis=0)
        return both[:, :head_size], both[:, head_size:]

    def halo_copy(h):
        return pltpu.make_async_remote_copy(
            src_ref=skv.at[h, rows(blocks - 1)], dst_ref=halo.at[h],
            send_sem=sh.at[h], recv_sem=rh.at[h],
            device_id={"seq": after}, device_id_type=MESH,
        )

    def back_copy(h):
        return pltpu.make_async_remote_copy(
            src_ref=back_send.at[h], dst_ref=back.at[h],
            send_sem=sb.at[h], recv_sem=rb.at[h],
            device_id={"seq": ahead}, device_id_type=MESH,
        )

    def each_head(f, first=0, last=heads):
        def go(h, _):
            f(h)
            return 0

        lax.fori_loop(first, last, go, 0)

    def pack_tokens(h):
        both = jnp.concatenate([qk_ref[:, cols(h)], v_ref[:, cols(h)]], axis=1)
        pack(out_row, h, both, send_x)

    def send_tokens(h):
        send_slots(h)
        pack_tokens(h)
        spread(send_x, recv_x, h, sx, rx)

    def sort_tokens(h):
        arrival_slots(h)
        wait_all(recv_x.at[h], rx.at[h])
        for b in range(blocks):
            arrived = unpack(in_col, h, b, recv_x)
            q = arrived[:, :head_size]
            sq[h, rows(b), :] = q.astype(BF16)
            skv[h, rows(b), :head_size] = (q * inverse_norm(q)).astype(BF16)
            skv[h, rows(b), head_size:] = arrived[:, head_size:].astype(BF16)
        halo_copy(h).start()
        grad = dot(og_ref[...], w_ref[cols(h), :], NT).astype(BF16)
        pack(out_row, h, grad, send_g)
        spread(send_g, recv_g, h, sg, rg)

    def attend(h):
        halo_copy(h).wait_recv()
        wait_all(recv_g.at[h], rg.at[h])
        outs = []
        for b in range(blocks):
            keys, vals = window(h, b)
            q = sq[h, rows(b), :]
            scores = dot(q, keys, NT) * scale
            own_id = lax.broadcasted_iota(jnp.int32, scores.shape, 0) + GROUP
            other = lax.broadcasted_iota(jnp.int32, scores.shape, 1)
            weights = jnp.where(own_id != other, jnp.exp(scores), 0.0)
            probability = (weights / jnp.sum(weights, axis=1, keepdims=True)).astype(BF16)
            outs.append(dot(probability, vals, NN).astype(BF16))
            grad = unpack(in_col, h, b, recv_g).astype(BF16)
            wide = probability.astype(F32)
            prob_grad = dot(grad, vals, NT)
            delta = jnp.sum(wide * prob_grad, axis=1, keepdims=True)
            score_grad = (wide * (prob_grad - delta) * scale).astype(BF16)
            acc_q[h, rows(b), :] = dot(score_grad, keys, NN)
            v_part = dot(probability, grad, TN)
            k_part = dot(score_grad, q, TN)
            if b == 0:
                back_send[h, :, :head_size] = k_part[:GROUP].astype(BF16)
                back_send[h, :, head_size:] = v_part[:GROUP].astype(BF16)
                back_copy(h).start()
            else:
                acc_k[h, rows(b - 1), :] += k_part[:GROUP]
                acc_v[h, rows(b - 1), :] += v_part[:GROUP]
            acc_k[h, rows(b), :] = k_part[GROUP:]
            acc_v[h, rows(b), :] = v_part[GROUP:]
        pack(in_row, h, jnp.concatenate(outs, axis=0), send_o)
        spread(send_o, recv_o, h, so, ro)

    def finish(h):
        back_copy(h).wait_recv()
        wait_sent(send_x, h, sx)
        done = []
        for b in range(blocks):
            k_grad = acc_k[h, rows(b), :]
            v_grad = acc_v[h, rows(b), :]
            if b == blocks - 1:
                k_grad += back[h, :, :head_size].astype(F32)
                v_grad += back[h, :, head_size:].astype(F32)
            q = sq[h, rows(b), :].astype(F32)
            norm = inverse_norm(q)
            inner = jnp.sum(k_grad * q, axis=1, keepdims=True) / head_size
            shared = acc_q[h, rows(b), :] + norm * k_grad - norm * norm * norm * inner * q
            done.append(jnp.concatenate([shared.astype(BF16), v_grad.astype(BF16)], axis=1))
        pack(in_row, h, jnp.concatenate(done, axis=0), send_x)
        spread(send_x, recv_d, h, sd, rd)

    def collect_out(h):
        wait_all(recv_o.at[h], ro.at[h])
        for b in range(blocks):
            att[rows(b), cols(h)] = unpack(out_col, h, b, recv_o).astype(BF16)

    def collect_grads(h):
        wait_all(recv_d.at[h], rd.at[h])
        for b in range(blocks):
            arrived = unpack(out_col, h, b, recv_d).astype(BF16)
            dqk_ref[rows(b), cols(h)] = arrived[:, :head_size]
            dv_ref[rows(b), cols(h)] = arrived[:, head_size:]
        for copy in grad_copies(h):
            copy.start()

    def grad_copies(h):
        at = (slice(None), cols(h))
        return (
            pltpu.make_async_copy(dqk_ref.at[at], dqk_out.at[at], oq.at[h]),
            pltpu.make_async_copy(dv_ref.at[at], dv_out.at[at], ov.at[h]),
        )

    send_slots(0)
    loads[0].wait()
    loads[1].wait()
    pack_tokens(0)
    pl.semaphore_wait(barrier, n - 1 + nh - 1)
    spread(send_x, recv_x, 0, sx, rx)
    each_head(send_tokens, 1)
    loads[2].wait()
    loads[3].wait()
    each_head(sort_tokens)
    early = heads // 2
    each_head(attend)
    each_head(finish, 0, early)
    each_head(collect_out)

    width = proj_ref.shape[1]
    tile = math.gcd(width, 256)

    def project(owner, write):
        def go(c, _):
            at = pl.multiple_of(c * tile, tile)
            taken = pl.ds(pl.multiple_of(owner * width + c * tile, tile), tile)
            write(pl.ds(at, tile), dot(att[...], w_ref[:, taken], NN))
            return 0

        lax.fori_loop(0, width // tile, go, 0)

    def part_copy(e):
        return pltpu.make_async_remote_copy(
            src_ref=part_send.at[e - 1], dst_ref=part_recv.at[e - 1],
            send_sem=sp.at[e - 1], recv_sem=rp.at[e - 1],
            device_id={"head": lax.rem(mh + e, nh)}, device_id_type=MESH,
        )

    for e in range(1, nh):
        def write_part(at, part, e=e):
            part_send[e - 1, :, at] = part.astype(BF16)

        project(lax.rem(mh + e, nh), write_part)
        part_copy(e).start()

    each_head(finish, early)

    def write_own(at, part):
        own[:, at] = part

    project(mh, write_own)
    each_head(collect_grads, 0, heads - 1)
    for e in range(1, nh):
        part_copy(e).wait_recv()
        own[...] += part_recv[e - 1].astype(F32)
    proj_ref[...] = own[...].astype(BF16)
    proj_copy = pltpu.make_async_copy(proj_ref, proj_out, op.at[0])
    proj_copy.start()
    collect_grads(heads - 1)

    def drain(h):
        for copy in grad_copies(h):
            copy.wait()
        wait_sent(send_x, h, sd)
        wait_sent(send_g, h, sg)
        wait_sent(send_o, h, so)
        halo_copy(h).wait_send()
        back_copy(h).wait_send()

    each_head(drain)
    for e in range(1, nh):
        part_copy(e).wait_send()
    proj_copy.wait()


def hand_over(*refs):
    half = len(refs) // 2
    for source, target in zip(refs[:half], refs[half:]):
        target[...] = source[...]


def on_device(query_key, values, out_weight, out_grad, sort_order, undo_order):
    tok_dev, flat_width = query_key.shape
    heads = sort_order.shape[0]
    head_size = flat_width // heads
    n = lax.axis_size("seq")
    nh = lax.axis_size("head")
    most = 3 * tok_dev // (2 * n)
    capacity = (most + 15) // 16 * 16
    slots = n * capacity
    width = out_weight.shape[1] // nh
    vmem = pl.BlockSpec(memory_space=pltpu.VMEM)
    sems = pltpu.SemaphoreType.DMA((heads,))
    anywhere = pl.BlockSpec(memory_space=pl.ANY)
    shape = jax.ShapeDtypeStruct
    results = pl.pallas_call(
        functools.partial(kernel, n, nh, capacity, head_size),
        out_shape=(
            shape((tok_dev, width), BF16),
            shape((tok_dev, flat_width), BF16),
            shape((tok_dev, flat_width), BF16),
        ),
        in_specs=[anywhere] * 4 + [vmem] * 2,
        out_specs=(anywhere,) * 3,
        scratch_shapes=[
            pltpu.VMEM(query_key.shape, BF16),
            pltpu.VMEM(values.shape, BF16),
            pltpu.VMEM(out_weight.shape, BF16),
            pltpu.VMEM(out_grad.shape, BF16),
            pltpu.VMEM((tok_dev, width), BF16),
            pltpu.VMEM((tok_dev, flat_width), BF16),
            pltpu.VMEM((tok_dev, flat_width), BF16),
            pltpu.VMEM((heads, 1, tok_dev), jnp.int32),
            pltpu.VMEM((tok_dev, heads), F32),
            pltpu.VMEM((heads, 1, tok_dev), jnp.int32),
            pltpu.VMEM((tok_dev, heads), F32),
            pltpu.VMEM((heads, slots, 2 * head_size), BF16),
            pltpu.VMEM((heads, slots, head_size), BF16),
            pltpu.VMEM((heads, slots, head_size), BF16),
            pltpu.VMEM((heads, slots, 2 * head_size), BF16),
            pltpu.VMEM((heads, slots, head_size), BF16),
            pltpu.VMEM((heads, slots, head_size), BF16),
            pltpu.VMEM((heads, slots, 2 * head_size), BF16),
            pltpu.VMEM((heads, tok_dev, head_size), BF16),
            pltpu.VMEM((heads, tok_dev, 2 * head_size), BF16),
            pltpu.VMEM((heads, GROUP, 2 * head_size), BF16),
            pltpu.VMEM((heads, tok_dev, head_size), F32),
            pltpu.VMEM((heads, tok_dev, head_size), F32),
            pltpu.VMEM((heads, tok_dev, head_size), F32),
            pltpu.VMEM((heads, GROUP, 2 * head_size), BF16),
            pltpu.VMEM((heads, GROUP, 2 * head_size), BF16),
            pltpu.VMEM((tok_dev, flat_width), BF16),
            pltpu.VMEM((max(nh - 1, 1), tok_dev, width), BF16),
            pltpu.VMEM((max(nh - 1, 1), tok_dev, width), BF16),
            pltpu.VMEM((tok_dev, width), F32),
        ]
        + [sems] * 14
        + [pltpu.SemaphoreType.DMA((max(nh - 1, 1),))] * 2
        + [pltpu.SemaphoreType.DMA((4,)), pltpu.SemaphoreType.DMA((1,))],
        compiler_params=pltpu.CompilerParams(
            collective_id=0, has_side_effects=True, vmem_limit_bytes=62 * 2**20
        ),
        cost_estimate=pl.CostEstimate(
            flops=2 * 10**10, bytes_accessed=2**24, transcendentals=2**21
        ),
    )(
        query_key, values, out_weight, out_grad, sort_order, undo_order
    )
    steps = 4

    def slab(r):
        return pl.BlockSpec((tok_dev // steps, r.shape[1]), lambda i: (i, 0))

    return pl.pallas_call(
        hand_over,
        grid=(steps,),
        out_shape=tuple(shape(r.shape, r.dtype) for r in results),
        in_specs=[slab(r) for r in results],
        out_specs=tuple(slab(r) for r in results),
        cost_estimate=pl.CostEstimate(
            flops=0, bytes_accessed=6 * values.size * 2, transcendentals=0
        ),
    )(*results)


def solution(mesh):
    placed = (
        P("seq", "head"),
        P("seq", "head"),
        P("head", None),
        P("seq", None),
        P("head", "seq"),
        P("head", "seq"),
    )
    return jax.shard_map(
        on_device,
        mesh=mesh,
        in_specs=placed,
        out_specs=(P("seq", "head"), P("seq", "head"), P("seq", "head")),
        check_vma=False,
    )
```

```python
import functools
import math

import jax
import jax.numpy as jnp
from jax import lax
from jax.experimental import pallas as pl
from jax.experimental.pallas import tpu as pltpu
from jax.sharding import PartitionSpec as P

GROUP = 256
NORM_EPS = 1e-06
MESH = pl.DeviceIdType.MESH
F32 = jnp.float32
BF16 = jnp.bfloat16


def quotient(x, by):
    return x >> (by.bit_length() - 1) if by & (by - 1) == 0 else lax.div(x, jnp.int32(by))


def dot(a, b, contract):
    return lax.dot_general(a, b, (contract, ((), ())), preferred_element_type=F32)


NN = ((1,), (0,))
NT = ((1,), (1,))
TN = ((0,), (0,))


def kernel(
    n, nh, capacity, head_size,
    qk_hbm, v_hbm, w_hbm, og_hbm, sort_ref, undo_ref,
    proj_out, dqk_out, dv_out,
    qk_ref, v_ref, w_ref, og_ref, proj_ref, dqk_ref, dv_ref,
    out_row, out_col, in_row, in_col,
    send_x, send_g, send_o, recv_x, recv_g, recv_o, recv_d,
    sq, skv, halo, acc_q, acc_k, acc_v, back_send, back,
    att, part_send, part_recv, own,
    sx, rx, sg, rg, so, ro, sd, rd, sh, rh, sb, rb, oq, ov, sp, rp, load, op,
):
    tok_dev, _ = qk_ref.shape
    heads = out_row.shape[0]
    slots = n * capacity
    step = math.gcd(slots, 256)
    blocks = tok_dev // GROUP
    scale = head_size ** (-0.5)
    me = lax.axis_index("seq")
    mh = lax.axis_index("head")
    after = lax.rem(me + 1, n)
    ahead = lax.rem(me + n - 1, n)

    barrier = pltpu.get_barrier_semaphore()

    def greet(d, _):
        pl.semaphore_signal(
            barrier, inc=1, device_id={"seq": lax.rem(me + d, n)}, device_id_type=MESH
        )
        return 0

    lax.fori_loop(1, n, greet, 0)
    for e in range(1, nh):
        pl.semaphore_signal(
            barrier, inc=1, device_id={"head": lax.rem(mh + e, nh)}, device_id_type=MESH
        )
    loads = [
        pltpu.make_async_copy(src, dst, load.at[i])
        for i, (src, dst) in enumerate(
            [(qk_hbm, qk_ref), (v_hbm, v_ref), (w_hbm, w_ref), (og_hbm, og_ref)]
        )
    ]
    for copy in loads[:2]:
        copy.start()
    out_col[...] = jnp.zeros_like(out_col)
    in_col[...] = jnp.zeros_like(in_col)

    def cols(h):
        return pl.ds(pl.multiple_of(h * head_size, head_size), head_size)

    def rows(b):
        return pl.ds(b * GROUP, GROUP)

    def spread(src, dst, h, send_sem, recv_sem):
        mine = pl.ds(pl.multiple_of(me * capacity, 16), capacity)

        def one(i, _):
            peer = lax.rem(me + i // 2 + (i % 2) * (n // 2), n)
            pltpu.make_async_remote_copy(
                src_ref=src.at[h, pl.ds(pl.multiple_of(peer * capacity, 16), capacity)],
                dst_ref=dst.at[h, mine],
                send_sem=send_sem.at[h],
                recv_sem=recv_sem.at[h],
                device_id={"seq": peer},
                device_id_type=MESH,
            ).start()
            return 0

        lax.fori_loop(1, n, one, 0)
        pltpu.make_async_copy(src.at[h, mine], dst.at[h, mine], recv_sem.at[h]).start()

    def wait_all(ref, sem):
        pltpu.make_async_copy(ref, ref, sem).wait()

    def wait_sent(src, h, sem):
        wait_all(src.at[h, pl.ds(0, slots - capacity)], sem.at[h])

    def pack(row_table, h, values, dst):
        places = row_table[h]
        for c in range(slots // step):
            ids = lax.broadcasted_iota(jnp.int32, (step, tok_dev), 0) + c * step
            pick = jnp.where(ids == places, 1.0, 0.0).astype(BF16)
            dst[h, pl.ds(c * step, step), :] = dot(pick, values, NN).astype(BF16)

    square = (tok_dev, tok_dev)

    def down():
        return lax.broadcasted_iota(jnp.int32, square, 0)

    def across():
        return lax.broadcasted_iota(jnp.int32, square, 1)

    def count(mask, axis):
        return jnp.sum(jnp.where(mask, 1.0, 0.0), axis=axis, keepdims=True)

    def as_column(row):
        picked = jnp.where(down() == across(), row.astype(F32), 0.0)
        return jnp.sum(picked, axis=1, keepdims=True).astype(jnp.int32)

    def put(row_table, col_table, h, row, col):
        row_table[h] = row.astype(jnp.int32)
        lane = lax.broadcasted_iota(jnp.int32, col_table.shape, 1)
        col_table[...] = jnp.where(lane == h, col, col_table[...])

    def send_slots(h):
        row = undo_ref[pl.ds(h, 1), :]
        col = as_column(row)
        to_row, to_col = quotient(row, tok_dev), quotient(col, tok_dev)
        same = to_row == to_col
        put(
            out_row, out_col, h,
            (to_row * capacity).astype(F32) + count(same & (col < row), 0),
            (to_col * capacity).astype(F32) + count(same & (row < col), 1),
        )

    def arrival_slots(h):
        row = quotient(sort_ref[pl.ds(h, 1), :], tok_dev)
        col = as_column(row)
        same = row == col
        put(
            in_row, in_col, h,
            (row * capacity).astype(F32) + count(same & (down() < across()), 0),
            (col * capacity).astype(F32) + count(same & (across() < down()), 1),
        )

    def column(col_table, h, b):
        table = col_table[rows(b), :]
        lane = lax.broadcasted_iota(jnp.int32, table.shape, 1)
        return jnp.sum(jnp.where(lane == h, table, 0.0), axis=1, keepdims=True).astype(jnp.int32)

    def unpack(col_table, h, b, src):
        ids = lax.broadcasted_iota(jnp.int32, (GROUP, slots), 1)
        pick = jnp.where(ids == column(col_table, h, b), 1.0, 0.0).astype(BF16)
        return dot(pick, src[h], NN)

    def inverse_norm(q):
        return lax.rsqrt(jnp.mean(q * q, axis=1, keepdims=True) + NORM_EPS)

    def window(h, b):
        prior = halo[h] if b == 0 else skv[h, rows(b - 1), :]
        both = jnp.concatenate([prior, skv[h, rows(b), :]], axis=0)
        return both[:, :head_size], both[:, head_size:]

    def halo_copy(h):
        return pltpu.make_async_remote_copy(
            src_ref=skv.at[h, rows(blocks - 1)], dst_ref=halo.at[h],
            send_sem=sh.at[h], recv_sem=rh.at[h],
            device_id={"seq": after}, device_id_type=MESH,
        )

    def back_copy(h):
        return pltpu.make_async_remote_copy(
            src_ref=back_send.at[h], dst_ref=back.at[h],
            send_sem=sb.at[h], recv_sem=rb.at[h],
            device_id={"seq": ahead}, device_id_type=MESH,
        )

    def each_head(f, first=0, last=heads):
        def go(h, _):
            f(h)
            return 0

        lax.fori_loop(first, last, go, 0)

    def pack_tokens(h):
        both = jnp.concatenate([qk_ref[:, cols(h)], v_ref[:, cols(h)]], axis=1)
        pack(out_row, h, both, send_x)

    def send_tokens(h):
        send_slots(h)
        pack_tokens(h)
        spread(send_x, recv_x, h, sx, rx)

    def sort_tokens(h):
        arrival_slots(h)
        wait_all(recv_x.at[h], rx.at[h])
        for b in range(blocks):
            arrived = unpack(in_col, h, b, recv_x)
            q = arrived[:, :head_size]
            sq[h, rows(b), :] = q.astype(BF16)
            skv[h, rows(b), :head_size] = (q * inverse_norm(q)).astype(BF16)
            skv[h, rows(b), head_size:] = arrived[:, head_size:].astype(BF16)
        halo_copy(h).start()
        grad = dot(og_ref[...], w_ref[cols(h), :], NT).astype(BF16)
        pack(out_row, h, grad, send_g)
        spread(send_g, recv_g, h, sg, rg)

    def attend(h):
        halo_copy(h).wait_recv()
        wait_all(recv_g.at[h], rg.at[h])
        outs = []
        for b in range(blocks):
            keys, vals = window(h, b)
            q = sq[h, rows(b), :]
            scores = dot(q, keys, NT) * scale
            own_id = lax.broadcasted_iota(jnp.int32, scores.shape, 0) + GROUP
            other = lax.broadcasted_iota(jnp.int32, scores.shape, 1)
            weights = jnp.where(own_id != other, jnp.exp(scores), 0.0)
            probability = (weights * (1.0 / jnp.sum(weights, axis=1, keepdims=True))).astype(BF16)
            outs.append(dot(probability, vals, NN).astype(BF16))
            grad = unpack(in_col, h, b, recv_g).astype(BF16)
            wide = probability.astype(F32)
            prob_grad = dot(grad, vals, NT)
            delta = jnp.sum(wide * prob_grad, axis=1, keepdims=True)
            score_grad = (wide * (prob_grad - delta) * scale).astype(BF16)
            acc_q[h, rows(b), :] = dot(score_grad, keys, NN)
            v_part = dot(probability, grad, TN)
            k_part = dot(score_grad, q, TN)
            if b == 0:
                back_send[h, :, :head_size] = k_part[:GROUP].astype(BF16)
                back_send[h, :, head_size:] = v_part[:GROUP].astype(BF16)
                back_copy(h).start()
            else:
                acc_k[h, rows(b - 1), :] += k_part[:GROUP]
                acc_v[h, rows(b - 1), :] += v_part[:GROUP]
            acc_k[h, rows(b), :] = k_part[GROUP:]
            acc_v[h, rows(b), :] = v_part[GROUP:]
        pack(in_row, h, jnp.concatenate(outs, axis=0), send_o)
        spread(send_o, recv_o, h, so, ro)

    def finish(h):
        back_copy(h).wait_recv()
        wait_sent(send_x, h, sx)
        done = []
        for b in range(blocks):
            k_grad = acc_k[h, rows(b), :]
            v_grad = acc_v[h, rows(b), :]
            if b == blocks - 1:
                k_grad += back[h, :, :head_size].astype(F32)
                v_grad += back[h, :, head_size:].astype(F32)
            q = sq[h, rows(b), :].astype(F32)
            norm = inverse_norm(q)
            inner = jnp.sum(k_grad * q, axis=1, keepdims=True) / head_size
            shared = acc_q[h, rows(b), :] + norm * k_grad - norm * norm * norm * inner * q
            done.append(jnp.concatenate([shared.astype(BF16), v_grad.astype(BF16)], axis=1))
        pack(in_row, h, jnp.concatenate(done, axis=0), send_x)
        spread(send_x, recv_d, h, sd, rd)

    def collect_out(h):
        wait_all(recv_o.at[h], ro.at[h])
        for b in range(blocks):
            att[rows(b), cols(h)] = unpack(out_col, h, b, recv_o).astype(BF16)

    def collect_grads(h):
        wait_all(recv_d.at[h], rd.at[h])
        for b in range(blocks):
            arrived = unpack(out_col, h, b, recv_d).astype(BF16)
            dqk_ref[rows(b), cols(h)] = arrived[:, :head_size]
            dv_ref[rows(b), cols(h)] = arrived[:, head_size:]
        for copy in grad_copies(h):
            copy.start()

    def grad_copies(h):
        at = (slice(None), cols(h))
        return (
            pltpu.make_async_copy(dqk_ref.at[at], dqk_out.at[at], oq.at[h]),
            pltpu.make_async_copy(dv_ref.at[at], dv_out.at[at], ov.at[h]),
        )

    send_slots(0)
    loads[0].wait()
    loads[1].wait()
    for copy in loads[2:]:
        copy.start()
    pack_tokens(0)
    pl.semaphore_wait(barrier, n - 1 + nh - 1)
    spread(send_x, recv_x, 0, sx, rx)
    early = heads // 2
    late = heads - early

    def send_and_sort(h):
        send_tokens(h + early)
        sort_tokens(h)

    def sort_and_attend(h):
        sort_tokens(h)
        attend(h - late)

    each_head(send_tokens, 1, early)
    loads[2].wait()
    loads[3].wait()
    each_head(send_and_sort, 0, late)
    each_head(sort_and_attend, late)
    each_head(attend, early)
    each_head(finish, 0, early)
    each_head(collect_out)

    width = proj_ref.shape[1]
    tile = math.gcd(width, 256)

    def project(owner, write):
        def go(c, _):
            at = pl.multiple_of(c * tile, tile)
            taken = pl.ds(pl.multiple_of(owner * width + c * tile, tile), tile)
            write(pl.ds(at, tile), dot(att[...], w_ref[:, taken], NN))
            return 0

        lax.fori_loop(0, width // tile, go, 0)

    def part_copy(e):
        return pltpu.make_async_remote_copy(
            src_ref=part_send.at[e - 1], dst_ref=part_recv.at[e - 1],
            send_sem=sp.at[e - 1], recv_sem=rp.at[e - 1],
            device_id={"head": lax.rem(mh + e, nh)}, device_id_type=MESH,
        )

    for e in range(1, nh):
        def write_part(at, part, e=e):
            part_send[e - 1, :, at] = part.astype(BF16)

        project(lax.rem(mh + e, nh), write_part)
        part_copy(e).start()

    each_head(finish, early)

    def write_own(at, part):
        own[:, at] = part

    project(mh, write_own)
    each_head(collect_grads, 0, heads - 1)
    for e in range(1, nh):
        part_copy(e).wait_recv()
        own[...] += part_recv[e - 1].astype(F32)
    proj_ref[...] = own[...].astype(BF16)
    proj_copy = pltpu.make_async_copy(proj_ref, proj_out, op.at[0])
    proj_copy.start()
    collect_grads(heads - 1)

    def drain(h):
        for copy in grad_copies(h):
            copy.wait()
        wait_sent(send_x, h, sd)
        wait_sent(send_g, h, sg)
        wait_sent(send_o, h, so)
        halo_copy(h).wait_send()
        back_copy(h).wait_send()

    each_head(drain)
    for e in range(1, nh):
        part_copy(e).wait_send()
    proj_copy.wait()


def hand_over(steps, *refs):
    *refs, loaded, stored = refs
    count = len(refs) // 3
    loads, stores = [], []
    for i in range(count):
        source, target, held = refs[i], refs[count + i], refs[2 * count + i]
        length = source.shape[0] // steps
        for c in range(steps):
            at = pl.ds(c * length, length)
            own = i * steps + c
            loads.append(pltpu.make_async_copy(source.at[at], held.at[at], loaded.at[own]))
            stores.append(pltpu.make_async_copy(held.at[at], target.at[at], stored.at[own]))
    for load in loads:
        load.start()
    for load, store in zip(loads, stores):
        load.wait()
        store.start()
    for store in stores:
        store.wait()


def on_device(query_key, values, out_weight, out_grad, sort_order, undo_order):
    tok_dev, flat_width = query_key.shape
    heads = sort_order.shape[0]
    head_size = flat_width // heads
    n = lax.axis_size("seq")
    nh = lax.axis_size("head")
    most = 3 * tok_dev // (2 * n)
    capacity = (most + 15) // 16 * 16
    slots = n * capacity
    width = out_weight.shape[1] // nh
    vmem = pl.BlockSpec(memory_space=pltpu.VMEM)
    sems = pltpu.SemaphoreType.DMA((heads,))
    anywhere = pl.BlockSpec(memory_space=pl.ANY)
    shape = jax.ShapeDtypeStruct
    results = pl.pallas_call(
        functools.partial(kernel, n, nh, capacity, head_size),
        out_shape=(
            shape((tok_dev, width), BF16),
            shape((tok_dev, flat_width), BF16),
            shape((tok_dev, flat_width), BF16),
        ),
        in_specs=[anywhere] * 4 + [vmem] * 2,
        out_specs=(anywhere,) * 3,
        scratch_shapes=[
            pltpu.VMEM(query_key.shape, BF16),
            pltpu.VMEM(values.shape, BF16),
            pltpu.VMEM(out_weight.shape, BF16),
            pltpu.VMEM(out_grad.shape, BF16),
            pltpu.VMEM((tok_dev, width), BF16),
            pltpu.VMEM((tok_dev, flat_width), BF16),
            pltpu.VMEM((tok_dev, flat_width), BF16),
            pltpu.VMEM((heads, 1, tok_dev), jnp.int32),
            pltpu.VMEM((tok_dev, heads), F32),
            pltpu.VMEM((heads, 1, tok_dev), jnp.int32),
            pltpu.VMEM((tok_dev, heads), F32),
            pltpu.VMEM((heads, slots, 2 * head_size), BF16),
            pltpu.VMEM((heads, slots, head_size), BF16),
            pltpu.VMEM((heads, slots, head_size), BF16),
            pltpu.VMEM((heads, slots, 2 * head_size), BF16),
            pltpu.VMEM((heads, slots, head_size), BF16),
            pltpu.VMEM((heads, slots, head_size), BF16),
            pltpu.VMEM((heads, slots, 2 * head_size), BF16),
            pltpu.VMEM((heads, tok_dev, head_size), BF16),
            pltpu.VMEM((heads, tok_dev, 2 * head_size), BF16),
            pltpu.VMEM((heads, GROUP, 2 * head_size), BF16),
            pltpu.VMEM((heads, tok_dev, head_size), F32),
            pltpu.VMEM((heads, tok_dev, head_size), F32),
            pltpu.VMEM((heads, tok_dev, head_size), F32),
            pltpu.VMEM((heads, GROUP, 2 * head_size), BF16),
            pltpu.VMEM((heads, GROUP, 2 * head_size), BF16),
            pltpu.VMEM((tok_dev, flat_width), BF16),
            pltpu.VMEM((max(nh - 1, 1), tok_dev, width), BF16),
            pltpu.VMEM((max(nh - 1, 1), tok_dev, width), BF16),
            pltpu.VMEM((tok_dev, width), F32),
        ]
        + [sems] * 14
        + [pltpu.SemaphoreType.DMA((max(nh - 1, 1),))] * 2
        + [pltpu.SemaphoreType.DMA((4,)), pltpu.SemaphoreType.DMA((1,))],
        compiler_params=pltpu.CompilerParams(
            collective_id=0, has_side_effects=True, vmem_limit_bytes=62 * 2**20
        ),
        cost_estimate=pl.CostEstimate(
            flops=2 * 10**10, bytes_accessed=2**24, transcendentals=2**21
        ),
    )(
        query_key, values, out_weight, out_grad, sort_order, undo_order
    )
    steps = 4
    return pl.pallas_call(
        functools.partial(hand_over, steps),
        out_shape=tuple(shape(r.shape, r.dtype) for r in results),
        in_specs=[anywhere] * 3,
        out_specs=(anywhere,) * 3,
        scratch_shapes=[pltpu.VMEM(r.shape, r.dtype) for r in results]
        + [pltpu.SemaphoreType.DMA((3 * steps,))] * 2,
        compiler_params=pltpu.CompilerParams(vmem_limit_bytes=60 * 2**20),
        cost_estimate=pl.CostEstimate(
            flops=0, bytes_accessed=6 * values.size * 2, transcendentals=0
        ),
    )(*results)


def solution(mesh):
    placed = (
        P("seq", "head"),
        P("seq", "head"),
        P("head", None),
        P("seq", None),
        P("head", "seq"),
        P("head", "seq"),
    )
    return jax.shard_map(
        on_device,
        mesh=mesh,
        in_specs=placed,
        out_specs=(P("seq", "head"), P("seq", "head"), P("seq", "head")),
        check_vma=False,
    )
```
